32 devices in a mesh: freq: 2 (over core), dir: 4 (over y, x), ap: 4 (over z).
Axes of the slice: x: 2, y: 2, z: 4, core: 2. Of those that a mesh axis runs over, the one named last changes fastest.
Arguments:
- signal: bfloat16 [2, 16384, 2048], P(None, 'ap', ('freq', 'dir')), parts along dimension 2, may hold values from -6 to 6
- positions: int32 [2, 16384], P(None, 'ap'), may hold values from 0 to 255
- weights: bfloat16 [4, 2, 2, 2, 256, 256], replicated, may hold values from -0.1875 to 0.1875
- directions: int32 [2, 16, 4096], P(None, 'ap', 'dir'), may hold values from 0 to 255
Outputs:
- beams: bfloat16 [2, 16, 4096, 2048], P(None, 'ap', 'dir', 'freq'), parts along dimension 3
The draws below stay inside these ranges and needn't reach their ends.
There are 2 independent parts, one for each index of `freq`. The reference program is written for one: setup_inputs(seed, part) draws one part's arguments, and reference() takes and returns one part's arrays. A program takes and returns all parts, laid end to end along the dimension named above; an argument that names none is the same for every part. Nothing has to cross between parts.
All inputs are finite; a program needn't handle non-finite values.
Results may differ from the reference program's by a relative error of at most 0.009.
Values may be sent and summed in bfloat16 or wider, within the bound.
A program may use at most 128 MiB of HBM per device.

```python
import math
import jax
import jax.numpy as jnp
from jax import lax

K = 256
EB = 256
GRID = 256
LEVELS = 4
Q = 4096
SNAP = 32
ABOX = 16
NE = 16384
BINS = 32


def plant(values, stream_key, low, top_value):
    longest = values.shape.index(max(values.shape))
    spots = []
    for shift in (0, 1):
        where = [jax.random.randint(jax.random.fold_in(stream_key, axis), (), 0, length) for axis, length in enumerate(values.shape)]
        where[longest] = (where[longest] + shift) % values.shape[longest]
        spots.append(tuple(where))
    return values.at[spots[0]].set(low).at[spots[1]].set(top_value)


def levels(rng, dims, cuts, least, high):
    level, own = 1.0, jax.random.fold_in(rng, 6)
    for axis_at, parts in cuts:
        heights = jnp.exp(jax.random.uniform(jax.random.fold_in(own, axis_at), (parts,), jnp.float32, least / len(cuts), high / len(cuts)))
        level = level * jnp.repeat(heights, dims[axis_at] // parts).reshape([-1 if axis == axis_at else 1 for axis in range(len(dims))])
    return level


def scatter_about(stream_key, shape, scale, bound, cuts=(), held_as=jnp.bfloat16):
    drawn = jax.random.normal(stream_key, shape, jnp.float32) * scale
    if len(cuts) > 0:
        drawn = levels(stream_key, shape, cuts, -0.22, 0.18) * drawn
    return jnp.clip(drawn, min=-bound, max=bound).astype(held_as)


def setup_inputs(seed: int = 0, part: int = 0) -> dict:
    seeds = jax.random.split(jax.random.key(seed), 5)
    own_keys = jax.random.split(jax.random.fold_in(seeds[4], part), 5)
    signal = scatter_about(own_keys[0], (2, NE, BINS * SNAP), 1.0, 6.0, ((1, 4), (2, 4)))
    positions = plant(jax.random.randint(seeds[1], (2, NE), 0, GRID), jax.random.fold_in(seeds[1], 1), 0, GRID - 1).astype(jnp.int32)
    weights = scatter_about(seeds[2], (LEVELS, 2, 2, 2, K, K), (4 * K) ** -0.5, 0.1875)
    directions = plant(jax.random.randint(seeds[3], (2, ABOX, Q), 0, GRID), jax.random.fold_in(seeds[3], 1), 0, GRID - 1).astype(jnp.int32)
    return {"signal": signal, "positions": positions, "weights": weights, "directions": directions}


def rounded(values):
    return lax.optimization_barrier(values.astype(jnp.bfloat16))

def wave_table(element_x_position, coord_y, side, factor):
    wavenumber_index = jnp.arange(side * side, dtype=jnp.int32)
    wave_x = wavenumber_index // side - side // 2
    wave_y = wavenumber_index % side - side // 2
    phase_int = jnp.mod(element_x_position[..., None] * wave_x + coord_y[..., None] * wave_y, GRID)
    angle_rad = phase_int.astype(jnp.float32) * (2.0 * math.pi / GRID)
    return (jnp.cos(angle_rad) * factor, jnp.sin(angle_rad) * factor)

def group_phase(per_box, side):
    tile_rows = 1 << per_box.bit_length() // 2
    tile_columns = per_box // tile_rows
    group_index = jnp.arange(per_box, dtype=jnp.int32)
    centre_x = group_index % tile_rows * (GRID // tile_rows)
    centre_y = group_index // tile_rows * (GRID // tile_columns)
    return wave_table(centre_x, centre_y, side, 1.0)

def element_table(element_x_position, coord_y, side):
    cosine, sine_part = wave_table(element_x_position, coord_y, side, 1.0 / math.sqrt(EB))
    row_real = jnp.stack([cosine, sine_part], -3)
    row_imag = jnp.stack([-sine_part, cosine], -3)
    return jnp.stack([row_real, row_imag], -4)

def direction_table(element_x_position, coord_y, side):
    cosine, sine_part = wave_table(element_x_position, coord_y, side, 1.0 / math.sqrt(K))
    row_real = jnp.stack([cosine, -sine_part], -2)
    row_imag = jnp.stack([sine_part, cosine], -2)
    return jnp.stack([row_real, row_imag], -4)

def expand(level_pair):
    w_real = level_pair[:, 0]
    w_imag = level_pair[:, 1]
    upper_rows = jnp.stack([w_real, -w_imag], 1)
    lower_rows = jnp.stack([w_imag, w_real], 1)
    block_matrix = jnp.stack([upper_rows, lower_rows], 0).transpose(0, 3, 1, 2, 4)
    return block_matrix.reshape(2 * K, 4 * K)

def reference(signal, positions, weights, directions):
    side = math.isqrt(K)
    all_boxes = NE // EB
    columns = signal.shape[2]
    boxes_data = signal.reshape(2, all_boxes, EB, columns).transpose(1, 0, 2, 3)
    element_x_position = positions[0].reshape(all_boxes, EB)
    coord_y = positions[1].reshape(all_boxes, EB)

    def leaf_box(items):
        signal_samples, box_x, box_y = items
        phase_table = rounded(element_table(box_x, box_y, side))
        beam_output = jnp.einsum('vdhn,dhy->vny', phase_table.astype(jnp.float32), signal_samples.astype(jnp.float32))
        return rounded(beam_output)
    coeffs = lax.map(leaf_box, (boxes_data, element_x_position, coord_y))
    for level_id in range(LEVELS):
        stride = all_boxes >> level_id + 1
        grouped_boxes = coeffs.astype(jnp.float32).reshape(all_boxes // (2 * stride), 2, stride, 2 * K, columns)
        joined = grouped_boxes.transpose(0, 2, 1, 3, 4).reshape(all_boxes // (2 * stride), stride, 4 * K, columns)
        results = []
        for parity in range(2):
            block_matrix = expand(weights[level_id, parity]).astype(jnp.float32)
            results.append(jnp.einsum('ij,ghjc->ghic', block_matrix, joined))
        coeffs = rounded(jnp.stack(results, 1).reshape(all_boxes, 2, K, columns))
    per_box = all_boxes // ABOX
    cosine, sine_part = group_phase(per_box, side)
    cosine = cosine[:, :, None]
    sine_part = sine_part[:, :, None]
    grouped_boxes = coeffs.astype(jnp.float32).reshape(ABOX, per_box, 2, K, columns)
    real_part = grouped_boxes[:, :, 0] * cosine + grouped_boxes[:, :, 1] * sine_part
    imag_part = grouped_boxes[:, :, 1] * cosine - grouped_boxes[:, :, 0] * sine_part
    summed = jnp.stack([lax.optimization_barrier(jnp.sum(real_part, axis=1)), lax.optimization_barrier(jnp.sum(imag_part, axis=1))], 1)
    summed = rounded(summed * (1.0 / math.sqrt(per_box)))

    def evaluate_box(items):
        coeff_box, steer_x, steer_y = items
        phase_table = rounded(direction_table(steer_x, steer_y, side))
        beam_output = jnp.einsum('oqik,ikc->oqc', phase_table.astype(jnp.float32), coeff_box.astype(jnp.float32))
        return beam_output.astype(jnp.bfloat16)
    beam_values = lax.map(evaluate_box, (summed, directions[0], directions[1]))
    return beam_values.transpose(1, 0, 2, 3)
```

```python
import functools
import math

import jax
import jax.numpy as jnp
from jax import lax
from jax.experimental import pallas as pl
from jax.experimental.pallas import tpu as pltpu
from jax.sharding import PartitionSpec as P

K = 256
EB = 256
GRID = 256
LEVELS = 4
ABOX = 16
SIDE = math.isqrt(K)
MESH = pl.DeviceIdType.MESH
MIB = 1 << 20


def log2(n):
    return n.bit_length() - 1


def dot(a, b):
    return jnp.dot(a, b, preferred_element_type=jnp.float32)


def classes(per_box):
    rx = 1 << per_box.bit_length() // 2
    return rx, per_box // rx


def wave_rows(x, y, factor):
    n = x.shape[-1]
    w = lax.broadcasted_iota(jnp.int32, (SIDE, n), 0) - SIDE // 2
    step = 2.0 * math.pi / GRID
    ax = ((w * x) & (GRID - 1)).astype(jnp.float32) * step
    ay = ((w * y) & (GRID - 1)).astype(jnp.float32) * step
    cx, sx = jnp.cos(ax)[:, None, :] * factor, jnp.sin(ax)[:, None, :] * factor
    cy, sy = jnp.cos(ay)[None, :, :], jnp.sin(ay)[None, :, :]
    c = (cx * cy - sx * sy).reshape(K, n).astype(jnp.bfloat16)
    s = (sx * cy + cx * sy).reshape(K, n).astype(jnp.bfloat16)
    return c, s


def to_natural(per_box):
    rx, ry = classes(per_box)
    hx, hy = SIDE // rx, SIDE // ry
    row = lax.broadcasted_iota(jnp.int32, (K, K), 0)
    col = lax.broadcasted_iota(jnp.int32, (K, K), 1)
    y_high = row & (hy - 1)
    x_high = (row >> log2(hy)) & (hx - 1)
    cls = row >> (log2(hx) + log2(hy))
    y_low = cls & (ry - 1)
    x_low = cls >> log2(ry)
    natural = (x_high * rx + x_low) * SIDE + y_high * ry + y_low
    return jnp.where(col == natural, 1.0, 0.0).astype(jnp.bfloat16)


def leaf_kernel(per_box, pos_ref, sig_ref, y_ref):
    rx, ry = classes(per_box)
    scale = 1.0 / math.sqrt(per_box)
    real, imag = [], []
    for m in range(per_box):
        c, s = wave_rows(pos_ref[0, 0, m : m + 1, :], pos_ref[1, 0, m : m + 1, :], 1.0 / math.sqrt(EB))
        sr = sig_ref[0, m * EB : (m + 1) * EB, :]
        si = sig_ref[1, m * EB : (m + 1) * EB, :]
        real.append(dot(c, sr) + dot(s, si))
        imag.append(dot(c, si) - dot(s, sr))
    for cls in range(per_box):
        wx, wy = cls // ry - SIDE // 2, cls % ry - SIDE // 2
        tr = ti = None
        for m in range(per_box):
            phase = (wx * (m % rx) * (GRID // rx) + wy * (m // rx) * (GRID // ry)) % GRID
            if phase * 4 % GRID == 0:
                cc, ss = ((1.0, 0.0), (0.0, 1.0), (-1.0, 0.0), (0.0, -1.0))[phase * 4 // GRID]
            else:
                cc, ss = math.cos(2 * math.pi * phase / GRID), math.sin(2 * math.pi * phase / GRID)
            for a, b in ((cc, ss),):
                r = [v * f for v, f in ((real[m], a), (imag[m], b)) if f != 0.0]
                i = [v * f for v, f in ((imag[m], a), (real[m], -b)) if f != 0.0]
                for v in r:
                    tr = v if tr is None else tr + v
                for v in i:
                    ti = v if ti is None else ti + v
        y_ref[cls, 0, 0:K, :] = (tr * scale).astype(jnp.bfloat16)
        y_ref[cls, 0, K : 2 * K, :] = (ti * scale).astype(jnp.bfloat16)


def cmul(a, b):
    r = dot(a[0], b[0]) - dot(a[1], b[1])
    i = dot(a[0], b[1]) + dot(a[1], b[0])
    return r.astype(jnp.bfloat16), i.astype(jnp.bfloat16)


def weights_kernel(per_box, nap, ap_ref, w_ref, v_ref, u_ref):
    nb = log2(nap)
    nloc = ABOX // nap
    kc = K // per_box
    ap = ap_ref[0]
    top = [None]
    for level in range(nb):
        c = (ap >> (nb - 1 - level)) & 1
        nxt = []
        for old in top:
            for r in range(2):
                w = (w_ref[level, r, c, 0], w_ref[level, r, c, 1])
                nxt.append(w if old is None else cmul(w, old))
        top = nxt
    for r, (re, im) in enumerate(top):
        v_ref[r, 0:K, 0:K] = re
        v_ref[r, 0:K, K:] = -im
        v_ref[r, K:, 0:K] = im
        v_ref[r, K:, K:] = re
    perm = to_natural(per_box)
    parts = {(0, 0): None}
    for level in range(nb, LEVELS):
        mats = {}
        for r in range(2):
            for c in range(2):
                w = (w_ref[level, r, c, 0], w_ref[level, r, c, 1])
                if level == LEVELS - 1:
                    w = tuple(dot(perm, part).astype(jnp.bfloat16) for part in w)
                mats[r, c] = w
        nxt = {}
        for (r0, c0), old in parts.items():
            for (r, c), w in mats.items():
                nxt[2 * r0 + r, 2 * c0 + c] = w if old is None else cmul(w, old)
        parts = nxt
    for (r, c), part in parts.items():
        re, im = (perm, jnp.zeros_like(perm)) if part is None else part
        for cls in range(per_box):
            rows = slice(cls * kc, (cls + 1) * kc)
            a, b = r * 2 * kc, c * 2 * K
            u_ref[cls, a : a + kc, b : b + K] = re[rows]
            u_ref[cls, a : a + kc, b + K : b + 2 * K] = -im[rows]
            u_ref[cls, a + kc : a + 2 * kc, b : b + K] = im[rows]
            u_ref[cls, a + kc : a + 2 * kc, b + K : b + 2 * K] = re[rows]


def exchange_kernel(
    per_box, nap, ndir, y_ref, v_ref, u_ref, z_ref,
    xs, acc, part, from_left, from_right,
    send_right, recv_right, send_left, recv_left, gather_send, gather_recv,
):
    nloc = ABOX // nap
    kc = K // per_box
    cols = y_ref.shape[-1]
    me = lax.axis_index("ap")
    col = lax.axis_index("dir")
    has_left, has_right = me > 0, me < nap - 1

    barrier = pltpu.get_barrier_semaphore()

    @pl.when(has_left)
    def _():
        pl.semaphore_signal(barrier, inc=1, device_id={"ap": me - 1}, device_id_type=MESH)

    @pl.when(has_right)
    def _():
        pl.semaphore_signal(barrier, inc=1, device_id={"ap": me + 1}, device_id_type=MESH)

    for p in range(1, ndir):
        pl.semaphore_signal(
            barrier, inc=1, device_id={"dir": lax.rem(col + p, ndir)}, device_id_type=MESH
        )

    on_line = has_left.astype(jnp.int32) + has_right.astype(jnp.int32)
    pl.semaphore_wait(barrier, ndir - 1 + on_line)

    def right_copy(dest, cls, slot):
        return pltpu.make_async_remote_copy(
            src_ref=part.at[dest, cls], dst_ref=from_left.at[dest, cls],
            send_sem=send_right.at[slot], recv_sem=recv_right.at[dest, cls],
            device_id={"ap": me + 1}, device_id_type=MESH,
        )

    def left_copy(dest, cls, slot):
        return pltpu.make_async_remote_copy(
            src_ref=part.at[dest, cls], dst_ref=from_right.at[dest, cls],
            send_sem=send_left.at[slot], recv_sem=recv_left.at[dest, cls],
            device_id={"ap": me - 1}, device_id_type=MESH,
        )

    def gather_copy(p, cls, sender):
        rows = pl.ds(pl.multiple_of(cls * kc, kc), kc)
        place = z_ref.at[sender, :, :, rows, :]
        return pltpu.make_async_remote_copy(
            src_ref=place, dst_ref=place,
            send_sem=gather_send.at[p, cls], recv_sem=gather_recv.at[sender, cls],
            device_id={"dir": lax.rem(col + p, ndir)}, device_id_type=MESH,
        )

    def finish(cls):
        acc[...] = part[me, cls].astype(jnp.float32)

        @pl.when(has_left)
        def _():
            right_copy(me, cls, 0).wait_recv()
            acc[...] += from_left[me, cls].astype(jnp.float32)

        @pl.when(has_right)
        def _():
            left_copy(me, cls, 0).wait_recv()
            acc[...] += from_right[me, cls].astype(jnp.float32)

        rows = pl.ds(pl.multiple_of(cls * kc, kc), kc)
        z_ref[col, :, :, rows, :] = acc[...].astype(jnp.bfloat16).reshape(nloc, 2, kc, cols)
        for p in range(1, ndir):
            gather_copy(p, cls, col).start()

    mirrored = me >= nap // 2
    low = jnp.where(mirrored, nap - 1 - me, me)
    extra = nap - 1 - 2 * low
    n_right, n_left = nap - 1 - me, me

    def step(t, carry):
        cls, q = t // nap, t % nap
        u = jnp.maximum(q - extra, 0)
        d = low - u // 2
        paired = jnp.where(u % 2 == 0, low - d, low + d)
        dest = jnp.where(q < extra, nap - 1 - q, paired)
        dest = jnp.where(mirrored, nap - 1 - dest, dest)
        going_right, going_left = dest > me, dest < me

        for c in range(nloc):
            xs[c * 2 * K : (c + 1) * 2 * K, :] = dot(v_ref[dest], y_ref[cls, c]).astype(jnp.bfloat16)
        acc[...] = dot(u_ref[cls], xs[...])

        @pl.when(going_right & has_left)
        def _():
            right_copy(dest, cls, 0).wait_recv()
            acc[...] += from_left[dest, cls].astype(jnp.float32)

        @pl.when(going_left & has_right)
        def _():
            left_copy(dest, cls, 0).wait_recv()
            acc[...] += from_right[dest, cls].astype(jnp.float32)

        part[dest, cls] = acc[...].astype(jnp.bfloat16)

        @pl.when(going_right)
        def _():
            number = cls * n_right + (nap - 1 - dest)

            @pl.when(number >= 2)
            def _():
                right_copy(dest, cls, number % 2).wait_send()

            right_copy(dest, cls, number % 2).start()

        @pl.when(going_left)
        def _():
            number = cls * n_left + dest

            @pl.when(number >= 2)
            def _():
                left_copy(dest, cls, number % 2).wait_send()

            left_copy(dest, cls, number % 2).start()

        @pl.when((q == nap - 1) & (cls > 0))
        def _():
            finish(cls - 1)

        return carry

    lax.fori_loop(0, per_box * nap, step, 0)
    finish(per_box - 1)
    for slot in range(2):
        @pl.when(has_right)
        def _():
            right_copy(0, 0, slot).wait_send()

        @pl.when(has_left)
        def _():
            left_copy(0, 0, slot).wait_send()

    for p in range(1, ndir):
        def drain(cls, carry, p=p):
            gather_copy(p, cls, col).wait_send()
            gather_copy(p, cls, lax.rem(col + p, ndir)).wait_recv()
            return carry

        lax.fori_loop(0, per_box, drain, 0)


def beam_kernel(per_box, dir_ref, z_ref, out_ref, zn):
    ndir = z_ref.shape[0]
    cols = z_ref.shape[-1]

    @pl.when(pl.program_id(1) == 0)
    def _():
        perm = to_natural(per_box)
        for d in range(ndir):
            for i in range(2):
                natural = lax.dot_general(
                    perm, z_ref[d, 0, i], (((0,), (0,)), ((), ())), preferred_element_type=jnp.float32
                )
                zn[i, :, d * cols : (d + 1) * cols] = natural.astype(jnp.bfloat16)

    c, s = wave_rows(dir_ref[0, 0, 0], dir_ref[1, 0, 0], 1.0 / math.sqrt(K))
    c, s = c.T, s.T
    out_ref[0, 0] = (dot(c, zn[0]) - dot(s, zn[1])).astype(jnp.bfloat16)
    out_ref[1, 0] = (dot(s, zn[0]) + dot(c, zn[1])).astype(jnp.bfloat16)


def local(nap, ndir, signal, positions, weights, directions):
    boxes = positions.shape[1] // EB
    cols = signal.shape[2]
    per_box = boxes * nap // ABOX
    nloc = ABOX // nap
    kc = K // per_box
    rows = nloc * 2 * kc
    bf16 = jnp.bfloat16
    vmem = pl.BlockSpec(memory_space=pltpu.VMEM)

    y = pl.pallas_call(
        functools.partial(leaf_kernel, per_box),
        grid=(nloc,),
        in_specs=[
            pl.BlockSpec((2, 1, per_box, EB), lambda g: (0, g, 0, 0)),
            pl.BlockSpec((2, per_box * EB, cols), lambda g: (0, g, 0)),
        ],
        out_specs=pl.BlockSpec((per_box, 1, 2 * K, cols), lambda g: (0, g, 0, 0)),
        out_shape=jax.ShapeDtypeStruct((per_box, nloc, 2 * K, cols), bf16),
        compiler_params=pltpu.CompilerParams(vmem_limit_bytes=48 * MIB),
        name="leaf",
    )(positions.reshape(2, nloc, per_box, EB), signal)

    v, u = pl.pallas_call(
        functools.partial(weights_kernel, per_box, nap),
        in_specs=[pl.BlockSpec(memory_space=pltpu.SMEM), vmem],
        out_specs=[vmem, vmem],
        out_shape=[
            jax.ShapeDtypeStruct((nap, 2 * K, 2 * K), bf16),
            jax.ShapeDtypeStruct((per_box, rows, nloc * 2 * K), bf16),
        ],
        compiler_params=pltpu.CompilerParams(vmem_limit_bytes=48 * MIB),
        name="weight_products",
    )(lax.axis_index("ap").reshape(1).astype(jnp.int32), weights)

    block = (nap, per_box, rows, cols)
    z = pl.pallas_call(
        functools.partial(exchange_kernel, per_box, nap, ndir),
        in_specs=[vmem] * 3,
        out_specs=vmem,
        out_shape=jax.ShapeDtypeStruct((ndir, nloc, 2, K, cols), bf16),
        scratch_shapes=[
            pltpu.VMEM((nloc * 2 * K, cols), bf16),
            pltpu.VMEM((rows, cols), jnp.float32),
            pltpu.VMEM(block, bf16),
            pltpu.VMEM(block, bf16),
            pltpu.VMEM(block, bf16),
            pltpu.SemaphoreType.DMA((2,)),
            pltpu.SemaphoreType.DMA((nap, per_box)),
            pltpu.SemaphoreType.DMA((2,)),
            pltpu.SemaphoreType.DMA((nap, per_box)),
            pltpu.SemaphoreType.DMA((ndir, per_box)),
            pltpu.SemaphoreType.DMA((ndir, per_box)),
        ],
        compiler_params=pltpu.CompilerParams(
            collective_id=0, has_side_effects=True, vmem_limit_bytes=58 * MIB
        ),
        name="exchange",
    )(y, v, u)

    qd = directions.shape[2]
    qb = min(256, qd)
    return pl.pallas_call(
        functools.partial(beam_kernel, per_box),
        grid=(nloc, qd // qb),
        in_specs=[
            pl.BlockSpec((2, 1, 1, 1, qb), lambda a, q: (0, a, q, 0, 0)),
            pl.BlockSpec((ndir, 1, 2, K, cols), lambda a, q: (0, a, 0, 0, 0)),
        ],
        out_specs=pl.BlockSpec((2, 1, qb, ndir * cols), lambda a, q: (0, a, q, 0)),
        out_shape=jax.ShapeDtypeStruct((2, nloc, qd, ndir * cols), bf16),
        scratch_shapes=[pltpu.VMEM((2, K, ndir * cols), bf16)],
        compiler_params=pltpu.CompilerParams(vmem_limit_bytes=48 * MIB),
        name="beams",
    )(directions.reshape(2, nloc, qd // qb, 1, qb), z)


def solution(mesh):
    in_specs = (P(None, "ap", ("freq", "dir")), P(None, "ap"), P(), P(None, "ap", "dir"))
    out_specs = P(None, "ap", "dir", "freq")
    fn = functools.partial(local, mesh.shape["ap"], mesh.shape["dir"])
    return jax.shard_map(fn, mesh=mesh, in_specs=in_specs, out_specs=out_specs, check_vma=False)
```

```python
import functools
import math

import jax
import jax.numpy as jnp
from jax import lax
from jax.experimental import pallas as pl
from jax.experimental.pallas import tpu as pltpu
from jax.sharding import PartitionSpec as P

K = 256
EB = 256
GRID = 256
LEVELS = 4
ABOX = 16
SIDE = math.isqrt(K)
MESH = pl.DeviceIdType.MESH
MIB = 1 << 20
SLOTS = 3


def log2(n):
    return n.bit_length() - 1


def dot(a, b):
    return jnp.dot(a, b, preferred_element_type=jnp.float32)


def classes(per_box):
    rx = 1 << per_box.bit_length() // 2
    return rx, per_box // rx


def wave_rows(x, y, factor):
    n = x.shape[-1]
    w = lax.broadcasted_iota(jnp.int32, (SIDE, n), 0) - SIDE // 2
    step = 2.0 * math.pi / GRID
    ax = ((w * x) & (GRID - 1)).astype(jnp.float32) * step
    ay = ((w * y) & (GRID - 1)).astype(jnp.float32) * step
    cx, sx = jnp.cos(ax)[:, None, :] * factor, jnp.sin(ax)[:, None, :] * factor
    cy, sy = jnp.cos(ay)[None, :, :], jnp.sin(ay)[None, :, :]
    c = (cx * cy - sx * sy).reshape(K, n).astype(jnp.bfloat16)
    s = (sx * cy + cx * sy).reshape(K, n).astype(jnp.bfloat16)
    return c, s


def to_natural(per_box):
    rx, ry = classes(per_box)
    hx, hy = SIDE // rx, SIDE // ry
    row = lax.broadcasted_iota(jnp.int32, (K, K), 0)
    col = lax.broadcasted_iota(jnp.int32, (K, K), 1)
    y_high = row & (hy - 1)
    x_high = (row >> log2(hy)) & (hx - 1)
    cls = row >> (log2(hx) + log2(hy))
    y_low = cls & (ry - 1)
    x_low = cls >> log2(ry)
    natural = (x_high * rx + x_low) * SIDE + y_high * ry + y_low
    return jnp.where(col == natural, 1.0, 0.0).astype(jnp.bfloat16)


def leaf_kernel(per_box, pos_ref, sig_ref, y_ref):
    rx, ry = classes(per_box)
    scale = 1.0 / math.sqrt(per_box)
    real, imag = [], []
    for m in range(per_box):
        c, s = wave_rows(pos_ref[0:1, m * EB : (m + 1) * EB], pos_ref[1:2, m * EB : (m + 1) * EB], 1.0 / math.sqrt(EB))
        sr = sig_ref[0, m * EB : (m + 1) * EB, :]
        si = sig_ref[1, m * EB : (m + 1) * EB, :]
        real.append(dot(c, sr) + dot(s, si))
        imag.append(dot(c, si) - dot(s, sr))
    for cls in range(per_box):
        wx, wy = cls // ry - SIDE // 2, cls % ry - SIDE // 2
        tr = ti = None
        for m in range(per_box):
            phase = (wx * (m % rx) * (GRID // rx) + wy * (m // rx) * (GRID // ry)) % GRID
            if phase * 4 % GRID == 0:
                cc, ss = ((1.0, 0.0), (0.0, 1.0), (-1.0, 0.0), (0.0, -1.0))[phase * 4 // GRID]
            else:
                cc, ss = math.cos(2 * math.pi * phase / GRID), math.sin(2 * math.pi * phase / GRID)
            for a, b in ((cc, ss),):
                r = [v * f for v, f in ((real[m], a), (imag[m], b)) if f != 0.0]
                i = [v * f for v, f in ((imag[m], a), (real[m], -b)) if f != 0.0]
                for v in r:
                    tr = v if tr is None else tr + v
                for v in i:
                    ti = v if ti is None else ti + v
        y_ref[cls, 0, 0:K, :] = (tr * scale).astype(jnp.bfloat16)
        y_ref[cls, 0, K : 2 * K, :] = (ti * scale).astype(jnp.bfloat16)


def cmul(a, b):
    r = dot(a[0], b[0]) - dot(a[1], b[1])
    i = dot(a[0], b[1]) + dot(a[1], b[0])
    return r.astype(jnp.bfloat16), i.astype(jnp.bfloat16)


def weights_kernel(per_box, nap, cuts, ap_ref, w_ref, v_ref, u_ref):
    nb = log2(nap)
    nloc = ABOX // nap
    kc = K // per_box
    ap = ap_ref[0]
    top = [None]
    for level in range(nb):
        c = (ap >> (nb - 1 - level)) & 1
        nxt = []
        for old in top:
            for r in range(2):
                w = (w_ref[level, r, c, 0], w_ref[level, r, c, 1])
                nxt.append(w if old is None else cmul(w, old))
        top = nxt
    for r, (re, im) in enumerate(top):
        v_ref[r, 0:K, 0:K] = re
        v_ref[r, 0:K, K:] = -im
        v_ref[r, K:, 0:K] = im
        v_ref[r, K:, K:] = re
    perm = to_natural(per_box)
    parts = {(0, 0): None}
    for level in range(nb, LEVELS):
        mats = {}
        for r in range(2):
            for c in range(2):
                w = (w_ref[level, r, c, 0], w_ref[level, r, c, 1])
                if level == LEVELS - 1:
                    w = tuple(dot(perm, part).astype(jnp.bfloat16) for part in w)
                mats[r, c] = w
        nxt = {}
        for (r0, c0), old in parts.items():
            for (r, c), w in mats.items():
                nxt[2 * r0 + r, 2 * c0 + c] = w if old is None else cmul(w, old)
        parts = nxt
    for (r, c), part in parts.items():
        re, im = (perm, jnp.zeros_like(perm)) if part is None else part
        each = nloc // cuts
        for cls in range(per_box):
            rows = slice(cls * kc, (cls + 1) * kc)
            chunk = cls * cuts + r // each
            a, b = r % each * 2 * kc, c * 2 * K
            u_ref[chunk, a : a + kc, b : b + K] = re[rows]
            u_ref[chunk, a : a + kc, b + K : b + 2 * K] = -im[rows]
            u_ref[chunk, a + kc : a + 2 * kc, b : b + K] = im[rows]
            u_ref[chunk, a + kc : a + 2 * kc, b + K : b + 2 * K] = re[rows]


def exchange_kernel(
    per_box, nap, ndir, cuts, qb, y_ref, v_ref, u_ref, dir_ref, z_ref, e_ref,
    xs, acc, part, from_left, from_right,
    send_right, recv_right, send_left, recv_left, gather_send, gather_recv,
):
    nloc = ABOX // nap
    each = nloc // cuts
    chunks = per_box * cuts
    kc = K // per_box
    cols = y_ref.shape[-1]
    me = lax.axis_index("ap")
    col = lax.axis_index("dir")
    has_left, has_right = me > 0, me < nap - 1

    barrier = pltpu.get_barrier_semaphore()

    @pl.when(has_left)
    def _():
        pl.semaphore_signal(barrier, inc=1, device_id={"ap": me - 1}, device_id_type=MESH)

    @pl.when(has_right)
    def _():
        pl.semaphore_signal(barrier, inc=1, device_id={"ap": me + 1}, device_id_type=MESH)

    for p in range(1, ndir):
        pl.semaphore_signal(
            barrier, inc=1, device_id={"dir": lax.rem(col + p, ndir)}, device_id_type=MESH
        )

    on_line = has_left.astype(jnp.int32) + has_right.astype(jnp.int32)
    pl.semaphore_wait(barrier, ndir - 1 + on_line)

    def right_copy(dest, cls, slot):
        return pltpu.make_async_remote_copy(
            src_ref=part.at[dest, cls], dst_ref=from_left.at[dest, cls],
            send_sem=send_right.at[slot], recv_sem=recv_right.at[dest, cls],
            device_id={"ap": me + 1}, device_id_type=MESH,
        )

    def left_copy(dest, cls, slot):
        return pltpu.make_async_remote_copy(
            src_ref=part.at[dest, cls], dst_ref=from_right.at[dest, cls],
            send_sem=send_left.at[slot], recv_sem=recv_left.at[dest, cls],
            device_id={"ap": me - 1}, device_id_type=MESH,
        )

    def spot(cls):
        rows = pl.ds(pl.multiple_of(cls // cuts * kc, kc), kc)
        return pl.ds(cls % cuts * each, each), rows

    def gather_copy(p, cls, sender):
        boxes, rows = spot(cls)
        place = z_ref.at[sender, boxes, :, rows, :]
        return pltpu.make_async_remote_copy(
            src_ref=place, dst_ref=place,
            send_sem=gather_send.at[p, cls], recv_sem=gather_recv.at[sender, cls],
            device_id={"dir": lax.rem(col + p, ndir)}, device_id_type=MESH,
        )

    def finish(cls):
        acc[...] = part[me, cls].astype(jnp.float32)

        @pl.when(has_left)
        def _():
            right_copy(me, cls, 0).wait_recv()
            acc[...] += from_left[me, cls].astype(jnp.float32)

        @pl.when(has_right)
        def _():
            left_copy(me, cls, 0).wait_recv()
            acc[...] += from_right[me, cls].astype(jnp.float32)

        boxes, rows = spot(cls)
        z_ref[col, boxes, :, rows, :] = acc[...].astype(jnp.bfloat16).reshape(each, 2, kc, cols)
        for p in range(1, ndir):
            gather_copy(p, cls, col).start()

    mirrored = me >= nap // 2
    low = jnp.where(mirrored, nap - 1 - me, me)
    extra = nap - 1 - 2 * low
    n_right, n_left = nap - 1 - me, me

    blocks = e_ref.shape[0]
    per_dir = blocks // nloc
    every = chunks * nap // blocks

    def steer(b):
        box, lanes = b // per_dir, pl.ds(pl.multiple_of(b % per_dir * qb, qb), qb)
        tables = wave_rows(
            dir_ref[0, pl.ds(box, 1), lanes], dir_ref[1, pl.ds(box, 1), lanes], 1.0 / math.sqrt(K)
        )
        perm = to_natural(per_box)
        for i in range(2):
            turned = lax.dot_general(
                tables[i], perm, (((0,), (1,)), ((), ())), preferred_element_type=jnp.float32
            )
            e_ref[b, i] = turned.astype(jnp.bfloat16)

    def step(t, carry):
        cls, q = t // nap, t % nap
        u = jnp.maximum(q - extra, 0)
        d = low - u // 2
        paired = jnp.where(u % 2 == 0, low - d, low + d)
        dest = jnp.where(q < extra, nap - 1 - q, paired)
        dest = jnp.where(mirrored, nap - 1 - dest, dest)
        going_right, going_left = dest > me, dest < me

        @pl.when(cls % cuts == 0)
        def _():
            for c in range(nloc):
                x = dot(v_ref[dest], y_ref[cls // cuts, c])
                xs[dest, c * 2 * K : (c + 1) * 2 * K, :] = x.astype(jnp.bfloat16)

        acc[...] = dot(u_ref[cls], xs[dest])

        @pl.when(going_right & has_left)
        def _():
            right_copy(dest, cls, 0).wait_recv()
            acc[...] += from_left[dest, cls].astype(jnp.float32)

        @pl.when(going_left & has_right)
        def _():
            left_copy(dest, cls, 0).wait_recv()
            acc[...] += from_right[dest, cls].astype(jnp.float32)

        part[dest, cls] = acc[...].astype(jnp.bfloat16)

        @pl.when(going_right)
        def _():
            number = cls * n_right + (nap - 1 - dest)

            @pl.when(number >= SLOTS)
            def _():
                right_copy(dest, cls, number % SLOTS).wait_send()

            right_copy(dest, cls, number % SLOTS).start()

        @pl.when(going_left)
        def _():
            number = cls * n_left + dest

            @pl.when(number >= SLOTS)
            def _():
                left_copy(dest, cls, number % SLOTS).wait_send()

            left_copy(dest, cls, number % SLOTS).start()

        @pl.when((q == 1) & (cls > 0))
        def _():
            finish(cls - 1)

        @pl.when(t % every == every - 1)
        def _():
            steer(t // every)

        return carry

    lax.fori_loop(0, chunks * nap, step, 0)
    finish(chunks - 1)
    for slot in range(SLOTS):
        @pl.when(has_right)
        def _():
            right_copy(0, 0, slot).wait_send()

        @pl.when(has_left)
        def _():
            left_copy(0, 0, slot).wait_send()

    for p in range(1, ndir):
        def drain(cls, carry, p=p):
            gather_copy(p, cls, col).wait_send()
            gather_copy(p, cls, lax.rem(col + p, ndir)).wait_recv()
            return carry

        lax.fori_loop(0, chunks, drain, 0)


def beam_kernel(e_ref, z_ref, out_ref):
    cols = z_ref.shape[-1]
    blocks, qb = e_ref.shape[0], e_ref.shape[2]
    for b in range(blocks):
        c, s = e_ref[b, 0], e_ref[b, 1]
        tables = jnp.concatenate([c, -s], 1), jnp.concatenate([s, c], 1)
        for d in range(z_ref.shape[0]):
            coeffs = z_ref[d, 0].reshape(2 * K, cols)
            for i in range(2):
                beams = dot(tables[i], coeffs).astype(jnp.bfloat16)
                out_ref[i, 0, b * qb : (b + 1) * qb, d * cols : (d + 1) * cols] = beams


def local(nap, ndir, signal, positions, weights, directions):
    boxes = positions.shape[1] // EB
    cols = signal.shape[2]
    per_box = boxes * nap // ABOX
    nloc = ABOX // nap
    kc = K // per_box
    cuts = min(2, nloc)
    rows = nloc // cuts * 2 * kc
    bf16 = jnp.bfloat16
    vmem = pl.BlockSpec(memory_space=pltpu.VMEM)

    y = pl.pallas_call(
        functools.partial(leaf_kernel, per_box),
        grid=(nloc,),
        in_specs=[
            pl.BlockSpec((2, per_box * EB), lambda g: (0, g)),
            pl.BlockSpec((2, per_box * EB, cols), lambda g: (0, g, 0)),
        ],
        out_specs=pl.BlockSpec((per_box, 1, 2 * K, cols), lambda g: (0, g, 0, 0)),
        out_shape=jax.ShapeDtypeStruct((per_box, nloc, 2 * K, cols), bf16),
        compiler_params=pltpu.CompilerParams(vmem_limit_bytes=60 * MIB),
        name="leaf",
    )(positions, signal)

    v, u = pl.pallas_call(
        functools.partial(weights_kernel, per_box, nap, cuts),
        in_specs=[pl.BlockSpec(memory_space=pltpu.SMEM), vmem],
        out_specs=[vmem, vmem],
        out_shape=[
            jax.ShapeDtypeStruct((nap, 2 * K, 2 * K), bf16),
            jax.ShapeDtypeStruct((per_box * cuts, rows, nloc * 2 * K), bf16),
        ],
        compiler_params=pltpu.CompilerParams(vmem_limit_bytes=60 * MIB),
        name="weight_products",
    )(lax.axis_index("ap").reshape(1).astype(jnp.int32), weights)

    qd = directions.shape[2]
    qb = min(256, qd)
    per_dir = qd // qb
    block = (nap, per_box * cuts, rows, cols)
    z, e = pl.pallas_call(
        functools.partial(exchange_kernel, per_box, nap, ndir, cuts, qb),
        in_specs=[vmem] * 4,
        out_specs=[vmem] * 2,
        out_shape=[
            jax.ShapeDtypeStruct((ndir, nloc, 2, K, cols), bf16),
            jax.ShapeDtypeStruct((nloc * per_dir, 2, qb, K), bf16),
        ],
        scratch_shapes=[
            pltpu.VMEM((nap, nloc * 2 * K, cols), bf16),
            pltpu.VMEM((rows, cols), jnp.float32),
            pltpu.VMEM(block, bf16),
            pltpu.VMEM(block, bf16),
            pltpu.VMEM(block, bf16),
            pltpu.SemaphoreType.DMA((SLOTS,)),
            pltpu.SemaphoreType.DMA((nap, per_box * cuts)),
            pltpu.SemaphoreType.DMA((SLOTS,)),
            pltpu.SemaphoreType.DMA((nap, per_box * cuts)),
            pltpu.SemaphoreType.DMA((ndir, per_box * cuts)),
            pltpu.SemaphoreType.DMA((ndir, per_box * cuts)),
        ],
        compiler_params=pltpu.CompilerParams(
            collective_id=0, has_side_effects=True, vmem_limit_bytes=58 * MIB
        ),
        name="exchange",
    )(y, v, u, directions)

    group = min(2, per_dir)
    return pl.pallas_call(
        beam_kernel,
        grid=(nloc, per_dir // group),
        in_specs=[
            pl.BlockSpec((group, 2, qb, K), lambda a, q: (a * (per_dir // group) + q, 0, 0, 0)),
            pl.BlockSpec((ndir, 1, 2, K, cols), lambda a, q: (0, a, 0, 0, 0)),
        ],
        out_specs=pl.BlockSpec((2, 1, group * qb, ndir * cols), lambda a, q: (0, a, q, 0)),
        out_shape=jax.ShapeDtypeStruct((2, nloc, qd, ndir * cols), bf16),
        compiler_params=pltpu.CompilerParams(vmem_limit_bytes=60 * MIB),
        name="beams",
    )(e, z)


def solution(mesh):
    in_specs = (P(None, "ap", ("freq", "dir")), P(None, "ap"), P(), P(None, "ap", "dir"))
    out_specs = P(None, "ap", "dir", "freq")
    fn = functools.partial(local, mesh.shape["ap"], mesh.shape["dir"])
    return jax.shard_map(fn, mesh=mesh, in_specs=in_specs, out_specs=out_specs, check_vma=False)
```

```python
import functools
import math

import jax
import jax.numpy as jnp
from jax import lax
from jax.experimental import pallas as pl
from jax.experimental.pallas import tpu as pltpu
from jax.sharding import PartitionSpec as P

K = 256
EB = 256
GRID = 256
LEVELS = 4
ABOX = 16
SIDE = math.isqrt(K)
MESH = pl.DeviceIdType.MESH
MIB = 1 << 20
SLOTS = 4


def log2(n):
    return n.bit_length() - 1


def dot(a, b):
    return jnp.dot(a, b, preferred_element_type=jnp.float32)


def classes(per_box):
    rx = 1 << per_box.bit_length() // 2
    return rx, per_box // rx


def wave_rows(x, y, factor):
    n = x.shape[-1]
    w = lax.broadcasted_iota(jnp.int32, (SIDE, n), 0) - SIDE // 2
    step = 2.0 * math.pi / GRID
    ax = ((w * x) & (GRID - 1)).astype(jnp.float32) * step
    ay = ((w * y) & (GRID - 1)).astype(jnp.float32) * step
    cx, sx = jnp.cos(ax)[:, None, :] * factor, jnp.sin(ax)[:, None, :] * factor
    cy, sy = jnp.cos(ay)[None, :, :], jnp.sin(ay)[None, :, :]
    c = (cx * cy - sx * sy).reshape(K, n).astype(jnp.bfloat16)
    s = (sx * cy + cx * sy).reshape(K, n).astype(jnp.bfloat16)
    return c, s


def to_natural(per_box):
    rx, ry = classes(per_box)
    hx, hy = SIDE // rx, SIDE // ry
    row = lax.broadcasted_iota(jnp.int32, (K, K), 0)
    col = lax.broadcasted_iota(jnp.int32, (K, K), 1)
    y_high = row & (hy - 1)
    x_high = (row >> log2(hy)) & (hx - 1)
    cls = row >> (log2(hx) + log2(hy))
    y_low = cls & (ry - 1)
    x_low = cls >> log2(ry)
    natural = (x_high * rx + x_low) * SIDE + y_high * ry + y_low
    return jnp.where(col == natural, 1.0, 0.0).astype(jnp.bfloat16)


def leaf_kernel(per_box, pos_ref, sig_ref, y_ref):
    rx, ry = classes(per_box)
    scale = 1.0 / math.sqrt(per_box)
    real, imag = [], []
    for m in range(per_box):
        c, s = wave_rows(pos_ref[0:1, m * EB : (m + 1) * EB], pos_ref[1:2, m * EB : (m + 1) * EB], 1.0 / math.sqrt(EB))
        sr = sig_ref[0, m * EB : (m + 1) * EB, :]
        si = sig_ref[1, m * EB : (m + 1) * EB, :]
        both = jnp.concatenate([c, s], 0)
        with_real, with_imag = dot(both, sr), dot(both, si)
        real.append(with_real[:K] + with_imag[K:])
        imag.append(with_imag[:K] - with_real[K:])
    for cls in range(per_box):
        wx, wy = cls // ry - SIDE // 2, cls % ry - SIDE // 2
        tr = ti = None
        for m in range(per_box):
            phase = (wx * (m % rx) * (GRID // rx) + wy * (m // rx) * (GRID // ry)) % GRID
            if phase * 4 % GRID == 0:
                cc, ss = ((1.0, 0.0), (0.0, 1.0), (-1.0, 0.0), (0.0, -1.0))[phase * 4 // GRID]
            else:
                cc, ss = math.cos(2 * math.pi * phase / GRID), math.sin(2 * math.pi * phase / GRID)
            for a, b in ((cc, ss),):
                r = [v * f for v, f in ((real[m], a), (imag[m], b)) if f != 0.0]
                i = [v * f for v, f in ((imag[m], a), (real[m], -b)) if f != 0.0]
                for v in r:
                    tr = v if tr is None else tr + v
                for v in i:
                    ti = v if ti is None else ti + v
        y_ref[cls, 0, 0:K, :] = (tr * scale).astype(jnp.bfloat16)
        y_ref[cls, 0, K : 2 * K, :] = (ti * scale).astype(jnp.bfloat16)


def cmul(a, b):
    r = dot(a[0], b[0]) - dot(a[1], b[1])
    i = dot(a[0], b[1]) + dot(a[1], b[0])
    return r.astype(jnp.bfloat16), i.astype(jnp.bfloat16)


def weight_products(per_box, nap, cuts, ap, w_ref, v_ref, u_ref):
    nb = log2(nap)
    nloc = ABOX // nap
    kc = K // per_box
    top = [None]
    for level in range(nb):
        c = (ap >> (nb - 1 - level)) & 1
        nxt = []
        for old in top:
            for r in range(2):
                w = (w_ref[level, r, c, 0], w_ref[level, r, c, 1])
                nxt.append(w if old is None else cmul(w, old))
        top = nxt
    for r, (re, im) in enumerate(top):
        a = r * 2 * K
        v_ref[a : a + K, 0:K] = re
        v_ref[a : a + K, K:] = -im
        v_ref[a + K : a + 2 * K, 0:K] = im
        v_ref[a + K : a + 2 * K, K:] = re
    perm = to_natural(per_box)
    parts = {(0, 0): None}
    for level in range(nb, LEVELS):
        mats = {}
        for r in range(2):
            for c in range(2):
                w = (w_ref[level, r, c, 0], w_ref[level, r, c, 1])
                if level == LEVELS - 1:
                    w = tuple(dot(perm, part).astype(jnp.bfloat16) for part in w)
                mats[r, c] = w
        nxt = {}
        for (r0, c0), old in parts.items():
            for (r, c), w in mats.items():
                nxt[2 * r0 + r, 2 * c0 + c] = w if old is None else cmul(w, old)
        parts = nxt
    for (r, c), part in parts.items():
        re, im = (perm, jnp.zeros_like(perm)) if part is None else part
        for cls in range(per_box):
            rows = slice(cls * kc, (cls + 1) * kc)
            a, b = r * 2 * kc, c * 2 * K
            u_ref[cls, a : a + kc, b : b + K] = re[rows]
            u_ref[cls, a : a + kc, b + K : b + 2 * K] = -im[rows]
            u_ref[cls, a + kc : a + 2 * kc, b : b + K] = im[rows]
            u_ref[cls, a + kc : a + 2 * kc, b + K : b + 2 * K] = re[rows]


def exchange_kernel(
    per_box, nap, ndir, cuts, qb, y_ref, w_ref, dir_ref, z_ref, e_ref,
    v_ref, u_ref, xs, own, acc, part, from_left, from_right,
    send_right, recv_right, send_left, recv_left, gather_send, gather_recv,
):
    nloc = ABOX // nap
    each = nloc // cuts
    chunks = per_box * cuts
    kc = K // per_box
    size = each * 2 * kc
    cols = y_ref.shape[-1]
    me = lax.axis_index("ap")
    col = lax.axis_index("dir")
    has_left, has_right = me > 0, me < nap - 1

    barrier = pltpu.get_barrier_semaphore()

    @pl.when(has_left)
    def _():
        pl.semaphore_signal(barrier, inc=1, device_id={"ap": me - 1}, device_id_type=MESH)

    @pl.when(has_right)
    def _():
        pl.semaphore_signal(barrier, inc=1, device_id={"ap": me + 1}, device_id_type=MESH)

    for p in range(1, ndir):
        pl.semaphore_signal(
            barrier, inc=1, device_id={"dir": lax.rem(col + p, ndir)}, device_id_type=MESH
        )

    weight_products(per_box, nap, cuts, me, w_ref, v_ref, u_ref)
    on_line = has_left.astype(jnp.int32) + has_right.astype(jnp.int32)
    pl.semaphore_wait(barrier, ndir - 1 + on_line)

    def right_copy(dest, cls, slot):
        return pltpu.make_async_remote_copy(
            src_ref=part.at[dest, cls], dst_ref=from_left.at[dest, cls],
            send_sem=send_right.at[slot], recv_sem=recv_right.at[dest, cls],
            device_id={"ap": me + 1}, device_id_type=MESH,
        )

    def left_copy(dest, cls, slot):
        return pltpu.make_async_remote_copy(
            src_ref=part.at[dest, cls], dst_ref=from_right.at[dest, cls],
            send_sem=send_left.at[slot], recv_sem=recv_left.at[dest, cls],
            device_id={"ap": me - 1}, device_id_type=MESH,
        )

    def spot(cls):
        rows = pl.ds(pl.multiple_of(cls // cuts * kc, kc), kc)
        return pl.ds(cls % cuts * each, each), rows

    def gather_copy(p, cls, sender):
        boxes, rows = spot(cls)
        place = z_ref.at[sender, boxes, :, rows, :]
        return pltpu.make_async_remote_copy(
            src_ref=place, dst_ref=place,
            send_sem=gather_send.at[p, cls], recv_sem=gather_recv.at[sender, cls],
            device_id={"dir": lax.rem(col + p, ndir)}, device_id_type=MESH,
        )

    def finish(cls):
        acc[...] = part[me, cls].astype(jnp.float32)

        @pl.when(has_left)
        def _():
            right_copy(me, cls, 0).wait_recv()
            acc[...] += from_left[me, cls].astype(jnp.float32)

        @pl.when(has_right)
        def _():
            left_copy(me, cls, 0).wait_recv()
            acc[...] += from_right[me, cls].astype(jnp.float32)

        boxes, rows = spot(cls)
        z_ref[col, boxes, :, rows, :] = acc[...].astype(jnp.bfloat16).reshape(each, 2, kc, cols)
        for p in range(1, ndir):
            gather_copy(p, cls, col).start()

    mirrored = me >= nap // 2
    low = jnp.where(mirrored, nap - 1 - me, me)
    extra = nap - 1 - 2 * low
    n_right, n_left = nap - 1 - me, me

    blocks = e_ref.shape[0]
    per_dir = blocks // nloc
    every = chunks * nap // blocks

    def steer(b):
        box, lanes = b // per_dir, pl.ds(pl.multiple_of(b % per_dir * qb, qb), qb)
        tables = wave_rows(
            dir_ref[0, pl.ds(box, 1), lanes], dir_ref[1, pl.ds(box, 1), lanes], 1.0 / math.sqrt(K)
        )
        perm = to_natural(per_box)
        for i in range(2):
            turned = lax.dot_general(
                tables[i], perm, (((0,), (1,)), ((), ())), preferred_element_type=jnp.float32
            )
            e_ref[b, i] = turned.astype(jnp.bfloat16)

    def step(t, carry):
        cls, q = t // nap, t % nap
        u = jnp.maximum(q - extra, 0)
        d = low - u // 2
        paired = jnp.where(u % 2 == 0, low - d, low + d)
        dest = jnp.where(q < extra, nap - 1 - q, paired)
        dest = jnp.where(mirrored, nap - 1 - dest, dest)
        going_right, going_left = dest > me, dest < me

        @pl.when((cls % cuts == 0) & (q == 0))
        def _():
            for c in range(nloc):
                x = dot(v_ref[...], y_ref[cls // cuts, c]).astype(jnp.bfloat16)
                for r in range(nap):
                    xs[r, c * 2 * K : (c + 1) * 2 * K, :] = x[r * 2 * K : (r + 1) * 2 * K]

        @pl.when(cls % cuts == 0)
        def _():
            total = dot(u_ref[cls // cuts], xs[dest])
            for h in range(cuts):
                own[dest, h] = total[h * size : (h + 1) * size]

        acc[...] = own[dest, cls % cuts]

        @pl.when(going_right & has_left)
        def _():
            right_copy(dest, cls, 0).wait_recv()
            acc[...] += from_left[dest, cls].astype(jnp.float32)

        @pl.when(going_left & has_right)
        def _():
            left_copy(dest, cls, 0).wait_recv()
            acc[...] += from_right[dest, cls].astype(jnp.float32)

        part[dest, cls] = acc[...].astype(jnp.bfloat16)

        @pl.when(going_right)
        def _():
            number = cls * n_right + (nap - 1 - dest)

            @pl.when(number >= SLOTS)
            def _():
                right_copy(dest, cls, number % SLOTS).wait_send()

            right_copy(dest, cls, number % SLOTS).start()

        @pl.when(going_left)
        def _():
            number = cls * n_left + dest

            @pl.when(number >= SLOTS)
            def _():
                left_copy(dest, cls, number % SLOTS).wait_send()

            left_copy(dest, cls, number % SLOTS).start()

        @pl.when((q == 1) & (cls > 0))
        def _():
            finish(cls - 1)

        if chunks % every == 0:
            @pl.when(cls % every == every - 1)
            def _():
                steer(cls // every * nap + q)
        else:
            @pl.when(t % every == every - 1)
            def _():
                steer(t // every)

        return carry

    lax.fori_loop(0, chunks * nap, step, 0)
    finish(chunks - 1)
    for slot in range(SLOTS):
        @pl.when(has_right)
        def _():
            right_copy(0, 0, slot).wait_send()

        @pl.when(has_left)
        def _():
            left_copy(0, 0, slot).wait_send()

    for p in range(1, ndir):
        def drain(cls, carry, p=p):
            gather_copy(p, cls, col).wait_send()
            gather_copy(p, cls, lax.rem(col + p, ndir)).wait_recv()
            return carry

        lax.fori_loop(0, chunks, drain, 0)


def beam_kernel(e_ref, z_ref, out_ref):
    cols = z_ref.shape[-1]
    blocks, qb = e_ref.shape[0], e_ref.shape[2]
    tables = []
    for i in range(2):
        for b in range(blocks):
            c, s = e_ref[b, 0], e_ref[b, 1]
            tables.append(jnp.concatenate([s, c] if i else [c, -s], 1))
    tall = jnp.concatenate(tables, 0)
    for d in range(z_ref.shape[0]):
        beams = dot(tall, z_ref[d, 0].reshape(2 * K, cols)).astype(jnp.bfloat16)
        for i in range(2):
            rows = slice(i * blocks * qb, (i + 1) * blocks * qb)
            out_ref[i, 0, :, d * cols : (d + 1) * cols] = beams[rows]


def local(nap, ndir, signal, positions, weights, directions):
    boxes = positions.shape[1] // EB
    cols = signal.shape[2]
    per_box = boxes * nap // ABOX
    nloc = ABOX // nap
    kc = K // per_box
    cuts = min(2, nloc)
    rows = nloc // cuts * 2 * kc
    bf16 = jnp.bfloat16
    vmem = pl.BlockSpec(memory_space=pltpu.VMEM)

    y = pl.pallas_call(
        functools.partial(leaf_kernel, per_box),
        grid=(nloc,),
        in_specs=[
            pl.BlockSpec((2, per_box * EB), lambda g: (0, g)),
            pl.BlockSpec((2, per_box * EB, cols), lambda g: (0, g, 0)),
        ],
        out_specs=pl.BlockSpec((per_box, 1, 2 * K, cols), lambda g: (0, g, 0, 0)),
        out_shape=jax.ShapeDtypeStruct((per_box, nloc, 2 * K, cols), bf16),
        compiler_params=pltpu.CompilerParams(vmem_limit_bytes=60 * MIB),
        name="leaf",
    )(positions, signal)

    qd = directions.shape[2]
    qb = min(256, qd)
    per_dir = qd // qb
    block = (nap, per_box * cuts, rows, cols)
    z, e = pl.pallas_call(
        functools.partial(exchange_kernel, per_box, nap, ndir, cuts, qb),
        in_specs=[vmem] * 3,
        out_specs=[vmem] * 2,
        out_shape=[
            jax.ShapeDtypeStruct((ndir, nloc, 2, K, cols), bf16),
            jax.ShapeDtypeStruct((nloc * per_dir, 2, qb, K), bf16),
        ],
        scratch_shapes=[
            pltpu.VMEM((nap * 2 * K, 2 * K), bf16),
            pltpu.VMEM((per_box, cuts * rows, nloc * 2 * K), bf16),
            pltpu.VMEM((nap, nloc * 2 * K, cols), bf16),
            pltpu.VMEM((nap, cuts, rows, cols), jnp.float32),
            pltpu.VMEM((rows, cols), jnp.float32),
            pltpu.VMEM(block, bf16),
            pltpu.VMEM(block, bf16),
            pltpu.VMEM(block, bf16),
            pltpu.SemaphoreType.DMA((SLOTS,)),
            pltpu.SemaphoreType.DMA((nap, per_box * cuts)),
            pltpu.SemaphoreType.DMA((SLOTS,)),
            pltpu.SemaphoreType.DMA((nap, per_box * cuts)),
            pltpu.SemaphoreType.DMA((ndir, per_box * cuts)),
            pltpu.SemaphoreType.DMA((ndir, per_box * cuts)),
        ],
        compiler_params=pltpu.CompilerParams(
            collective_id=0, has_side_effects=True, vmem_limit_bytes=58 * MIB
        ),
        name="exchange",
    )(y, weights, directions)

    group = min(2, per_dir)
    return pl.pallas_call(
        beam_kernel,
        grid=(nloc, per_dir // group),
        in_specs=[
            pl.BlockSpec((group, 2, qb, K), lambda a, q: (a * (per_dir // group) + q, 0, 0, 0)),
            pl.BlockSpec((ndir, 1, 2, K, cols), lambda a, q: (0, a, 0, 0, 0)),
        ],
        out_specs=pl.BlockSpec((2, 1, group * qb, ndir * cols), lambda a, q: (0, a, q, 0)),
        out_shape=jax.ShapeDtypeStruct((2, nloc, qd, ndir * cols), bf16),
        compiler_params=pltpu.CompilerParams(vmem_limit_bytes=60 * MIB),
        name="beams",
    )(e, z)


def solution(mesh):
    in_specs = (P(None, "ap", ("freq", "dir")), P(None, "ap"), P(), P(None, "ap", "dir"))
    out_specs = P(None, "ap", "dir", "freq")
    fn = functools.partial(local, mesh.shape["ap"], mesh.shape["dir"])
    return jax.shard_map(fn, mesh=mesh, in_specs=in_specs, out_specs=out_specs, check_vma=False)
```
